32 devices in a mesh: group: 2 (over y), ep: 16 (over z, x, core), tp: 1.
Axes of the slice: x: 2, y: 2, z: 4, core: 2. Of those that a mesh axis runs over, the one named last changes fastest.
Arguments:
- hidden_in: bfloat16 [2, 512, 3584], P(None, ('group', 'ep'), 'tp'), parts along dimension 1, may hold values from -16 to 16
- queries: bfloat16 [2, 512, 64, 576], P(None, ('group', 'ep'), 'tp'), parts along dimension 1, may hold values from -64 to 64
- new_latents: bfloat16 [2, 512, 576], P(None, ('group', 'ep')), parts along dimension 1, may hold values from -6 to 6
- cache: bfloat16 [384, 192, 576], P(('group', 'ep'), 'tp'), parts along dimension 0, may hold values from -8 to 8
- prefill_pool: bfloat16 [128, 192, 576], P(('group', 'ep'), 'tp'), parts along dimension 0, may hold values from -6 to 6
- requests: int32 [128], P(('group', 'ep')), parts along dimension 0, may hold values from 0 to 63, as said below
- context_len: int32 [512], P(('group', 'ep')), parts along dimension 0, may hold values from 48 to 192
- picks: int32 [2, 512, 8], P(None, ('group', 'ep')), parts along dimension 1, may hold values from 0 to 15, all different within a row; in each aligned block of 16 rows (0 to 15, 16 to 31, ..., all dimensions but the last counted through in order) at most 12 rows name the same one
- w_uv: bfloat16 [64, 512, 128], P('tp'), may hold values from -1 to 1
- w_out: bfloat16 [64, 128, 3584], P('tp'), may hold values from -0.0625 to 0.0625
- norm_gain: float32 [3584], replicated, may hold values from 0.1 to 1.9
- router: bfloat16 [3584, 16], replicated, may hold values from -0.09375 to 0.09375
- w_gate: bfloat16 [16, 3584, 1024], P('ep', None, 'tp'), may hold values from -0.09375 to 0.09375
- w_up: bfloat16 [16, 3584, 1024], P('ep', None, 'tp'), may hold values from -0.09375 to 0.09375
- w_down: bfloat16 [16, 1024, 3584], P('ep', 'tp'), may hold values from -0.1875 to 0.1875
Outputs:
- layer_out: bfloat16 [2, 512, 3584], P(None, ('group', 'ep'), 'tp'), parts along dimension 1
The draws below stay inside these ranges and needn't reach their ends.
There are 2 independent parts, one for each index of `group`. The reference program is written for one: setup_inputs(seed, part) draws one part's arguments, and reference() takes and returns one part's arrays. A program takes and returns all parts, laid end to end along the dimension named above; an argument that names none is the same for every part. Nothing has to cross between parts.
Inputs may be any that keep to these rules, and one draw needn't show every extreme that they name: `requests`: entry r * 4 + k names the prefill_pool row of the k-th new row of ep index r; every prefill_pool row is named exactly once; the 4 entries of one ep index name at most 1 row held by any one ep index, and some pair reaches 1. `picks`: in the rows of one ep index and one step, no expert is named by more than 12 rows, a bound that some block reaches.
All inputs are finite; a program needn't handle non-finite values.
Results may differ from the reference program's by a relative error of at most 0.012.
Values may be sent and summed in bfloat16 or wider, within the bound.
A program may use at most 192 MiB of HBM per device.

```python
import math
import jax
import jax.numpy as jnp
import numpy as np
from jax import lax

D = 3584
H = 64
LAT = 512
ROPE = 64
VD = 128
FF = 1024
STEPS = 2
ROW_DEV = 16
CTX = 192
EXPERTS = 16
TOP = 8
POOL_DEV = 4
RES_DEV = 12
CAP = 12
ROWS = 256
N_EP = 16


def draw_cache(key, part):
    key = jax.random.fold_in(key, 5)
    shape = (N_EP * RES_DEV, CTX, LAT + ROPE)
    base = jnp.clip(jax.random.normal(key, shape, jnp.float32), -6.0, 6.0)
    return base.astype(jnp.bfloat16)


def draw_queries(key, part):
    key = jax.random.fold_in(key, 9)
    shape = (STEPS, N_EP * ROW_DEV, H, LAT + ROPE)
    base = jnp.clip(jax.random.normal(key, shape, jnp.float32), -6.0, 6.0)
    return base.astype(jnp.bfloat16)


def draw_hidden_in(key, part):
    key = jax.random.fold_in(key, 13)
    first = jax.random.fold_in(key, 0)
    second = jax.random.fold_in(key, 1)
    fourth = jax.random.fold_in(key, 3)
    shape = (STEPS, N_EP * ROW_DEV, D)
    row_scale = jnp.exp(jax.random.uniform(first, (STEPS, N_EP * ROW_DEV, 1), jnp.float32, math.log(0.1), 0.0))
    col_scale = jnp.exp(jax.random.uniform(second, (D,), jnp.float32, math.log(0.5), math.log(2.0)))
    noise = jnp.clip(jax.random.normal(fourth, shape, jnp.float32), -6.0, 6.0)
    values = row_scale * noise * col_scale
    return values.astype(jnp.bfloat16)


def owner_order(key):
    return jax.random.permutation(key, POOL_DEV)


def draw_requests(key, part):
    key = jax.random.fold_in(key, 17)
    first, second, third, fourth = jax.random.split(key, 4)
    distinct = min(POOL_DEV, N_EP)
    shifts = jax.random.permutation(first, N_EP)[:distinct]
    inner = jax.random.permutation(second, N_EP)
    outer = jax.random.permutation(third, N_EP)
    orders = jax.vmap(owner_order)(jax.random.split(fourth, N_EP))
    asker = jnp.arange(N_EP)[:, None]
    column = jnp.arange(POOL_DEV)[None, :]
    owner = outer[(inner[asker] + shifts[column % distinct]) % N_EP]
    slot = orders[owner, column]
    return (owner * POOL_DEV + slot).reshape(-1).astype(jnp.int32)


def touch_ends(entries, own_key, least, top_value):
    shape = entries.shape
    place = [jax.random.randint(jax.random.fold_in(own_key, axis), (), 0, shape[axis]) for axis in range(len(shape))]
    entries = entries.at[tuple(place)].set(least)
    longest = shape.index(max(shape))
    place[longest] = (place[longest] + 1) % shape[longest]
    return entries.at[tuple(place)].set(top_value)


def block_scale(own_key, shape, pieces, low, high):
    level, own = 1.0, jax.random.fold_in(own_key, 6)
    for position, shards_of in pieces:
        steps = jnp.exp(jax.random.uniform(jax.random.fold_in(own, position), (shards_of,), jnp.float32, low / len(pieces), high / len(pieces)))
        level = level * jnp.repeat(steps, shape[position] // shards_of).reshape([-1 if axis == position else 1 for axis in range(len(shape))])
    return level


def shared_out(key, own, number, rows, count, top, most, slope):
    ranking = jax.random.permutation(key, count)
    heavy_load, usual = load_shares(count, rows * top, most, slope, True), load_shares(count, rows * top, most, slope, False)
    places = jnp.arange(count)

    def named(tallies, turn):
        used = int((tallies > 0).sum())
        fixed = max(1, used // 4)
        passed = fixed + (places - fixed + turn * (used - fixed)) % max(1, count - fixed)
        return jnp.zeros((count,), jnp.int32).at[ranking[jnp.where(places < fixed, places, passed)]].set(jnp.asarray(tallies, jnp.int32))

    tallies = jnp.where(number % 4 == 0, named(heavy_load, number // 4), named(usual, number - number // 4 - 1))
    mixed = jax.random.permutation(jax.random.fold_in(own, 3), count)
    giver, sink = mixed[0:count // 2 * 2:2], mixed[1:count // 2 * 2:2]
    margin = jnp.minimum(tallies[giver] - 1, most - tallies[sink]) // 2
    margin = jnp.where((giver == ranking[0]) | (sink == ranking[0]) | (tallies[sink] == 0), 0, jnp.maximum(margin, 0))
    passed = jax.random.randint(jax.random.fold_in(own, 4), (count // 2,), 0, 1 << 20) % (margin + 1)
    tallies = tallies.at[giver].add(-passed).at[sink].add(passed)
    items = jnp.searchsorted(jnp.cumsum(tallies), jnp.arange(rows * top), side="right").astype(jnp.int32)
    listing = items.reshape(top, rows).T
    listing = listing[jax.random.permutation(jax.random.fold_in(own, 1), rows)]
    turn = jax.random.randint(jax.random.fold_in(own, 2), (rows, 1), 0, top)
    return jnp.take_along_axis(listing, (jnp.arange(top)[None, :] + turn) % top, axis=1)


def load_shares(number_of, total, reach, lean, full):
    portions = [(1 << 20) // math.isqrt(standing ** lean) + 1 for standing in range(1, number_of + 1)]
    largest = reach if full else min(reach, max(-(-total // number_of), total * portions[0] // sum(portions)))
    least = 1 if total - largest >= number_of - 1 else 0
    given, spare = [largest] + [least] * (number_of - 1), total - largest - least * (number_of - 1)
    while spare > 0:
        free = [i for i in range(1, number_of) if given[i] < largest] or [i for i in range(1, number_of) if given[i] < reach]
        pool, remaining = sum([portions[i] for i in free]), spare
        for i in free:
            addition = min(reach - given[i], max(1, remaining * portions[i] // pool), spare)
            given[i] = given[i] + addition
            spare = spare - addition
    return np.array(given)


def normal_values(stream_key, shape, deviation, most, cuts=(), held_as=jnp.bfloat16):
    factor_of = block_scale(stream_key, shape, cuts, -0.22, 0.18) if cuts else 1.0
    values = jax.random.normal(stream_key, shape, jnp.float32) * deviation * factor_of
    return jnp.minimum(jnp.maximum(values, -most), most).astype(held_as)


def setup_inputs(seed: int = 0, part: int = 0) -> dict:
    arg_keys = jax.random.split(jax.random.key(seed), 16)
    own_keys = jax.random.split(jax.random.fold_in(arg_keys[15], part), 16)
    hidden_in = draw_hidden_in(jax.random.fold_in(jax.random.fold_in(arg_keys[15], part), 71), part)
    queries = draw_queries(jax.random.fold_in(jax.random.fold_in(arg_keys[15], part), 71), part)
    new_latents = normal_values(own_keys[2], (STEPS, ROWS, LAT + ROPE), 1.0, 6.0, ((1, 16),))
    cache = draw_cache(jax.random.fold_in(jax.random.fold_in(arg_keys[15], part), 71), part)
    prefill_pool = normal_values(own_keys[4], (N_EP * POOL_DEV, CTX, LAT + ROPE), 1.0, 6.0, ((0, 16),))
    requests = draw_requests(jax.random.fold_in(jax.random.fold_in(arg_keys[15], part), 71), part)
    context_len = touch_ends(jax.random.randint(own_keys[6], (ROWS,), max(2, CTX // 4), CTX + 1), jax.random.fold_in(own_keys[6], 1), max(2, CTX // 4), CTX).astype(jnp.int32)
    picks_keys = jax.random.split(jax.random.fold_in(own_keys[7], 1), STEPS * ROWS // ROW_DEV)
    picks_turns = jax.random.permutation(jax.random.fold_in(own_keys[7], 3), STEPS * ROWS // ROW_DEV)
    picks = jax.vmap(lambda own, number: shared_out(jax.random.fold_in(own_keys[7], 2), own, number, ROW_DEV, EXPERTS, TOP, CAP, 2))(picks_keys, picks_turns).reshape((STEPS, ROWS, TOP))
    w_uv = normal_values(arg_keys[8], (H, LAT, VD), (LAT // 16) ** -0.5, 1.0)
    w_out = normal_values(arg_keys[9], (H, VD, D), (H * VD) ** -0.5, 0.0625)
    norm_gain = jnp.clip(1.0 + 0.18 * jax.random.normal(arg_keys[10], (D,), jnp.float32), 0.1, 1.9)
    router = normal_values(arg_keys[11], (D, EXPERTS), D ** -0.5, 0.09375)
    w_gate = normal_values(arg_keys[12], (EXPERTS, D, FF), D ** -0.5, 0.09375, ((0, 16),))
    w_up = normal_values(arg_keys[13], (EXPERTS, D, FF), D ** -0.5, 0.09375, ((0, 16),))
    w_down = normal_values(arg_keys[14], (EXPERTS, FF, D), FF ** -0.5, 0.1875, ((0, 16),))
    return {"hidden_in": hidden_in, "queries": queries, "new_latents": new_latents, "cache": cache, "prefill_pool": prefill_pool, "requests": requests, "context_len": context_len, "picks": picks, "w_uv": w_uv, "w_out": w_out, "norm_gain": norm_gain, "router": router, "w_gate": w_gate, "w_up": w_up, "w_down": w_down}


SOFT_SCALE = 192.0 ** (-0.5)
ROUTE_SCALE = 2.5
NORM_EPS = 1e-06
NEG_FILL = -1e+30
EXACT = lax.Precision.HIGHEST

def assemble(cache, prefill_pool, requests):
    width = LAT + ROPE
    resident = cache.reshape(N_EP, RES_DEV, CTX, width)
    fetched = prefill_pool[requests].reshape(N_EP, POOL_DEV, CTX, width)
    return jnp.concatenate([resident, fetched], axis=1).reshape(N_EP * ROW_DEV, CTX, width)

def attend(query_step, keys, new_latents, context_len, step):
    queries = query_step.astype(jnp.float32)
    cached = keys.astype(jnp.float32)
    fresh = new_latents.astype(jnp.float32)
    scores = jnp.einsum('rhc,rjc->rhj', queries, cached, precision=EXACT) * SOFT_SCALE
    valid = jnp.arange(CTX)[None, :] < context_len[:, None]
    scores = jnp.where(valid[:, None, :], scores, NEG_FILL)
    extra = jnp.einsum('rhc,urc->rhu', queries, fresh, precision=EXACT) * SOFT_SCALE
    live = jnp.arange(STEPS) <= step
    extra = jnp.where(live[None, None, :], extra, NEG_FILL)
    peak = jnp.maximum(lax.optimization_barrier(jnp.max(scores, axis=-1)), lax.optimization_barrier(jnp.max(extra, axis=-1)))
    cache_weights = jnp.exp(scores - peak[..., None])
    fresh_weights = jnp.exp(extra - peak[..., None])
    total = lax.optimization_barrier(jnp.sum(cache_weights, axis=-1)) + lax.optimization_barrier(jnp.sum(fresh_weights, axis=-1))
    mixed = jnp.einsum('rhj,rjc->rhc', cache_weights, cached[:, :, :LAT], precision=EXACT)
    mixed = mixed + jnp.einsum('rhu,urc->rhc', fresh_weights, fresh[:, :, :LAT], precision=EXACT)
    return (mixed / total[..., None]).astype(jnp.bfloat16)

def expert_mix(normed, picks_step, gates, w_gate, w_up, w_down):
    limit = N_EP * CAP

    def visit(total, expert):
        chosen = picks_step == expert
        weight = lax.optimization_barrier(jnp.sum(jnp.where(chosen, gates, 0.0), axis=1))
        member = jnp.any(chosen, axis=1)
        order = jnp.argsort(jnp.where(member, 0, 1).astype(jnp.int32), stable=True)[:limit]
        rows = normed[order]
        gate = jnp.dot(rows, w_gate[expert], preferred_element_type=jnp.float32)
        upper = jnp.dot(rows, w_up[expert], preferred_element_type=jnp.float32)
        active = (jax.nn.silu(gate) * upper).astype(jnp.bfloat16)
        produced = jnp.dot(active, w_down[expert], preferred_element_type=jnp.float32)
        return (total.at[order].add(weight[order][:, None] * produced), None)
    start = jnp.zeros((normed.shape[0], D), jnp.float32)
    total, unused = lax.scan(visit, start, jnp.arange(EXPERTS).astype(jnp.int32))
    return total

def reference(hidden_in, queries, new_latents, cache, prefill_pool, requests, context_len, picks, w_uv, w_out, norm_gain, router, w_gate, w_up, w_down):
    keys = assemble(cache, prefill_pool, requests)
    results = []
    for step in range(STEPS):
        latent = attend(queries[step], keys, new_latents, context_len, step)
        values = jnp.einsum('rhc,hcv->rhv', latent.astype(jnp.float32), w_uv.astype(jnp.float32), precision=EXACT).astype(jnp.bfloat16)
        attended = jnp.einsum('rhv,hvd->rd', values.astype(jnp.float32), w_out.astype(jnp.float32), precision=EXACT)
        hidden = hidden_in[step].astype(jnp.float32) + attended
        scale = lax.rsqrt(lax.optimization_barrier(jnp.mean(hidden * hidden, axis=-1, keepdims=True)) + NORM_EPS)
        normed = (hidden * scale * norm_gain).astype(jnp.bfloat16)
        affinity = jax.nn.sigmoid(jnp.dot(normed, router, preferred_element_type=jnp.float32))
        chosen = jnp.take_along_axis(affinity, picks[step], axis=1)
        gates = chosen / lax.optimization_barrier(jnp.sum(chosen, axis=1, keepdims=True)) * ROUTE_SCALE
        mixed = expert_mix(normed, picks[step], gates, w_gate, w_up, w_down)
        results.append((hidden + mixed).astype(jnp.bfloat16))
    return jnp.stack(results)
```

```python
import jax
import jax.numpy as jnp
from jax import lax
from jax.sharding import PartitionSpec as P

LAT = 512

SOFT_SCALE = 192.0 ** (-0.5)
ROUTE_SCALE = 2.5
NORM_EPS = 1e-06
NEG_FILL = -1e30


def attend_rows(queries, new_latents, rows_cache, context_len):
    steps = queries.shape[0]
    fresh = (
        jnp.einsum("trhc,urc->trhu", queries, new_latents, preferred_element_type=jnp.float32)
        * SOFT_SCALE
    )
    live = jnp.arange(steps)[None, :] <= jnp.arange(steps)[:, None]
    fresh = jnp.where(live[:, None, None, :], fresh, NEG_FILL)
    scores = (
        jnp.einsum("trhc,rjc->trhj", queries, rows_cache, preferred_element_type=jnp.float32)
        * SOFT_SCALE
    )
    valid = jnp.arange(rows_cache.shape[1])[None, :] < context_len[:, None]
    scores = jnp.where(valid[None, :, None, :], scores, NEG_FILL)
    peak = jnp.maximum(jnp.max(fresh, axis=-1), jnp.max(scores, axis=-1))
    fresh_weights = jnp.exp(fresh - peak[..., None])
    weights = jnp.exp(scores - peak[..., None])
    total = jnp.sum(fresh_weights, axis=-1) + jnp.sum(weights, axis=-1)
    acc = jnp.einsum(
        "trhj,rjc->trhc",
        weights.astype(jnp.bfloat16),
        rows_cache[:, :, :LAT],
        preferred_element_type=jnp.float32,
    )
    for u in range(steps):
        acc = acc + fresh_weights[..., u, None] * new_latents[u, None, :, None, :LAT].astype(jnp.float32)
    return (acc / total[..., None]).astype(jnp.bfloat16)


def shards(
    hidden_in,
    queries,
    new_latents,
    cache,
    prefill_pool,
    requests,
    context_len,
    picks,
    w_uv,
    w_out,
    norm_gain,
    router,
    w_gate,
    w_up,
    w_down,
):
    n_ep = lax.axis_size("ep")
    me = lax.axis_index("ep")
    steps, rows, share = hidden_in.shape
    heads, width = queries.shape[2], queries.shape[3]
    res, pool, top = cache.shape[0], prefill_pool.shape[0], picks.shape[2]
    experts, model = router.shape[1], router.shape[0]
    bf16 = jnp.bfloat16

    small = jnp.concatenate([requests, context_len, picks.reshape(-1)])
    small = lax.all_gather(small, "ep", axis=0)
    req_all = small[:, :pool]
    ctx_all = small[:, pool : pool + rows]
    picks_all = small[:, pool + rows :].reshape(n_ep * steps * rows, top)

    extra = -(-share // width)
    moved_hidden = jnp.pad(hidden_in[:, res:], ((0, 0), (0, 0), (0, extra * width - share)))
    packed = jnp.concatenate(
        [
            queries[:, res:],
            new_latents[:, res:, None, :],
            moved_hidden.reshape(steps, pool, extra, width),
        ],
        axis=2,
    )
    to_owner = (jnp.arange(n_ep)[:, None] == (requests // pool)[None, :]).astype(bf16)
    outgoing = jnp.einsum("dk,tkhc->dthc", to_owner, packed, preferred_element_type=jnp.float32).astype(bf16)
    arrived = lax.all_to_all(outgoing, "ep", split_axis=0, concat_axis=0, tiled=True)
    own_slot = me * pool + jnp.arange(pool)
    asked = req_all[None] == own_slot[:, None, None]
    from_asker = jnp.any(asked, axis=2).astype(bf16)
    taken = jnp.einsum("pe,ethc->tphc", from_asker, arrived, preferred_element_type=jnp.float32).astype(bf16)
    moved_queries = taken[:, :, :heads]
    moved_latents = taken[:, :, heads]
    moved_hidden = taken[:, :, heads + 1 :].reshape(steps, pool, extra * width)[:, :, :share]
    moved_ctx = jnp.sum(jnp.where(asked, ctx_all[None, :, res:], 0), axis=(1, 2))

    if lax.axis_size("tp") > 1:
        cache = lax.all_gather(cache, "tp", axis=1, tiled=True)
        prefill_pool = lax.all_gather(prefill_pool, "tp", axis=1, tiled=True)
    latent = jnp.concatenate(
        [
            attend_rows(queries[:, :res], new_latents[:, :res], cache, context_len[:res]),
            attend_rows(moved_queries, moved_latents, prefill_pool, moved_ctx),
        ],
        axis=1,
    )
    values = jnp.einsum("trhc,hcv->trhv", latent, w_uv, preferred_element_type=jnp.float32).astype(bf16)
    partial_value = jnp.einsum("trhv,hvd->trd", values, w_out, preferred_element_type=jnp.float32)
    hidden_rows = jnp.concatenate([hidden_in[:, :res], moved_hidden], axis=1).astype(jnp.float32)
    tp = lax.axis_index("tp")
    if lax.axis_size("tp") > 1:
        column = tp * share
        placed = lax.dynamic_update_slice_in_dim(jnp.zeros_like(partial_value), hidden_rows, column, 2)
        hidden = lax.psum(partial_value + placed, "tp")
        own_cols = lax.dynamic_slice_in_dim(hidden, column, share, 2)
    else:
        hidden = partial_value + hidden_rows
        own_cols = hidden
    scale = lax.rsqrt(jnp.mean(hidden * hidden, axis=-1, keepdims=True) + NORM_EPS)
    normed = (hidden * scale * norm_gain).astype(bf16)

    gathered = lax.all_gather(normed.reshape(steps * rows, model), "ep", axis=0, tiled=True)
    total = n_ep * steps * rows
    by_ep = jnp.arange(n_ep)[:, None, None]
    by_step = jnp.arange(steps)[None, :, None]
    by_row = jnp.arange(rows)[None, None, :]
    asked_slot = jnp.concatenate([jnp.zeros((n_ep, res), jnp.int32), req_all], axis=1)[:, None, :]
    source_ep = jnp.where(by_row < res, by_ep, asked_slot // pool)
    source_row = jnp.where(by_row < res, by_row, res + asked_slot % pool)
    source = ((source_ep * steps + by_step) * rows + source_row).reshape(total)
    order = (source[:, None] == jnp.arange(total)[None, :]).astype(bf16)
    everyone = jnp.dot(order, gathered, preferred_element_type=jnp.float32).astype(bf16)

    affinity = jax.nn.sigmoid(jnp.dot(everyone, router, preferred_element_type=jnp.float32))
    member = jnp.any(picks_all[:, :, None] == jnp.arange(experts), axis=1)
    chosen = jnp.where(member, affinity, 0.0)
    mine = jnp.sum(jnp.where(jnp.arange(experts) == me, chosen, 0.0), axis=1)
    weight = mine / jnp.sum(chosen, axis=1) * ROUTE_SCALE

    gate = jnp.dot(everyone, w_gate[0], preferred_element_type=jnp.float32)
    upper = jnp.dot(everyone, w_up[0], preferred_element_type=jnp.float32)
    active = (jax.nn.silu(gate) * upper).astype(bf16)
    produced = jnp.dot(active, w_down[0], preferred_element_type=jnp.float32)


    local = jnp.arange(steps * pool)
    local_source = (me * steps + local // pool) * rows + res + local % pool
    back = (source[:, None] == local_source[None, :]).astype(bf16)
    moved_back = jnp.where(tp == 0, hidden[:, res:], 0.0).astype(bf16).reshape(steps * pool, model)
    returned = jnp.dot(back, moved_back, preferred_element_type=jnp.float32)
    contribution = (produced * weight[:, None] + returned).astype(bf16)

    summed = lax.psum_scatter(contribution, "ep", scatter_dimension=0, tiled=True)
    summed = summed.reshape(steps, rows, model)
    if lax.axis_size("tp") > 1:
        summed = lax.psum_scatter(summed, "tp", scatter_dimension=2, tiled=True)
    resident = jnp.arange(rows)[None, :, None] < res
    return (jnp.where(resident, own_cols, 0.0) + summed.astype(jnp.float32)).astype(bf16)


def solution(mesh):
    in_specs = (
        P(None, ("group", "ep"), "tp"),
        P(None, ("group", "ep"), "tp", None),
        P(None, ("group", "ep"), None),
        P(("group", "ep"), "tp", None),
        P(("group", "ep"), "tp", None),
        P(("group", "ep")),
        P(("group", "ep")),
        P(None, ("group", "ep"), None),
        P("tp", None, None),
        P("tp", None, None),
        P(),
        P(),
        P("ep", None, "tp"),
        P("ep", None, "tp"),
        P("ep", "tp", None),
    )
    out_specs = P(None, ("group", "ep"), "tp")
    return jax.shard_map(shards, mesh=mesh, in_specs=in_specs, out_specs=out_specs, check_vma=False)
```

```python
import functools

import jax
import jax.numpy as jnp
from jax import lax
from jax.experimental import pallas as pl
from jax.experimental.pallas import tpu as pltpu
from jax.sharding import PartitionSpec as P

LAT = 512

SOFT_SCALE = 192.0 ** (-0.5)
ROUTE_SCALE = 2.5
NORM_EPS = 1e-06
NEG_FILL = -1e30


def attend_rows(queries, new_latents, rows_cache, context_len):
    steps = queries.shape[0]
    fresh = (
        jnp.einsum("trhc,urc->trhu", queries, new_latents, preferred_element_type=jnp.float32)
        * SOFT_SCALE
    )
    live = jnp.arange(steps)[None, :] <= jnp.arange(steps)[:, None]
    fresh = jnp.where(live[:, None, None, :], fresh, NEG_FILL)
    scores = (
        jnp.einsum("trhc,rjc->trhj", queries, rows_cache, preferred_element_type=jnp.float32)
        * SOFT_SCALE
    )
    valid = jnp.arange(rows_cache.shape[1])[None, :] < context_len[:, None]
    scores = jnp.where(valid[None, :, None, :], scores, NEG_FILL)
    peak = jnp.maximum(jnp.max(fresh, axis=-1), jnp.max(scores, axis=-1))
    fresh_weights = jnp.exp(fresh - peak[..., None])
    weights = jnp.exp(scores - peak[..., None])
    total = jnp.sum(fresh_weights, axis=-1) + jnp.sum(weights, axis=-1)
    acc = jnp.einsum(
        "trhj,rjc->trhc",
        weights.astype(jnp.bfloat16),
        rows_cache[:, :, :LAT],
        preferred_element_type=jnp.float32,
    )
    for u in range(steps):
        acc = acc + fresh_weights[..., u, None] * new_latents[u, None, :, None, :LAT].astype(jnp.float32)
    return (acc / total[..., None]).astype(jnp.bfloat16)


def ring_kernel(
    n_ep, snake, block_ref, gate_hbm, up_hbm, down_hbm, out_ref,
    seen, made, from_twin, sums, half_sums, active, w_gate, w_up, w_down,
    send_sem, recv_sem, load_sem,
):
    chips = n_ep // 2
    me = lax.axis_index("ep")
    chip, core = me // 2, me % 2
    if snake:
        place = jnp.where(chip % 2 == 0, chip // 2, chips - 1 - chip // 2)
        at = lambda p: jnp.where(p < chips // 2, 2 * p, 2 * (chips - 1 - p) + 1)
    else:
        place = chip
        at = lambda p: p
    right = at((place + 1) % chips) * 2 + core
    left = at((place + chips - 1) % chips) * 2 + core
    twin = chip * 2 + 1 - core
    block, model = out_ref.shape
    half = block // 2
    chunk = 4 * block
    far = chips // 2

    barrier = pltpu.get_barrier_semaphore()
    for other in (left, right, twin):
        pl.semaphore_signal(barrier, inc=1, device_id={"ep": other}, device_id_type=pl.DeviceIdType.MESH)
    pl.semaphore_wait(barrier, 3)

    loads = [
        pltpu.make_async_copy(hbm.at[0], vmem, load_sem.at[i])
        for i, (hbm, vmem) in enumerate(((gate_hbm, w_gate), (up_hbm, w_up), (down_hbm, w_down)))
    ]
    copies = []

    def send(src, dst, to):
        k = len(copies)
        copy = pltpu.make_async_remote_copy(
            src_ref=src, dst_ref=dst, send_sem=send_sem.at[k], recv_sem=recv_sem.at[k],
            device_id={"ep": to}, device_id_type=pl.DeviceIdType.MESH,
        )
        copy.start()
        copies.append(copy)
        return copy

    def rows_of(ref, start, size):
        return ref.at[pl.ds(start, size), :]

    to_right = send(block_ref, rows_of(seen, chunk, block), right)
    to_left = send(block_ref, rows_of(seen, chunk + block, block), left)
    to_twin = [send(block_ref, rows_of(seen, 2 * block, block), twin)]
    for load in loads:
        load.start()
    seen[0:block, :] = block_ref[...]

    def experts(index):
        base = index * chunk
        f_tile = min(256, w_gate.shape[1])
        d_tile = 512 if model % 512 == 0 else 128

        @pl.loop(0, w_gate.shape[1] // f_tile)
        def _(i):
            columns = pl.ds(pl.multiple_of(i * f_tile, f_tile), f_tile)
            rows = seen[base : base + chunk, :model]
            gate = jnp.dot(rows, w_gate[:, columns], preferred_element_type=jnp.float32)
            upper = jnp.dot(rows, w_up[:, columns], preferred_element_type=jnp.float32)
            active[:, columns] = (gate / (1.0 + jnp.exp(-gate)) * upper).astype(active.dtype)

        carried = seen[base : base + chunk, model:].astype(jnp.float32)
        lane = lax.broadcasted_iota(jnp.int32, carried.shape, 1)
        weight = jnp.sum(jnp.where((lane == me) | (lane == me + n_ep), carried, 0.0), axis=1, keepdims=True)

        @pl.loop(0, model // d_tile)
        def _(i):
            columns = pl.ds(pl.multiple_of(i * d_tile, d_tile), d_tile)
            produced = jnp.dot(active[...], w_down[:, columns], preferred_element_type=jnp.float32)
            made[base : base + chunk, columns] = (produced * weight).astype(made.dtype)

    shared = []

    def share(index):
        shared.append(
            send(rows_of(made, index * chunk + 2 * block, 2 * block), rows_of(from_twin, index * 2 * block, 2 * block), twin)
        )

    for s in range(1, far):
        base = s * chunk
        to_right.wait_recv()
        if s < far - 1:
            to_right = send(rows_of(seen, base, block), rows_of(seen, base + chunk, block), right)
        else:
            to_right = send(rows_of(seen, base, half), rows_of(seen, block, half), right)
        to_left.wait_recv()
        if s < far - 1:
            to_left = send(rows_of(seen, base + block, block), rows_of(seen, base + chunk + block, block), left)
        else:
            to_left = send(rows_of(seen, base + block + half, half), rows_of(seen, block + half, half), left)
        both = send(rows_of(seen, base, 2 * block), rows_of(seen, base + 2 * block, 2 * block), twin)
        if s == 1:
            for load in loads:
                load.wait()
        both.wait_recv()
        experts(s)
        share(s)
    to_right.wait_recv()
    to_left.wait_recv()
    last = send(rows_of(seen, block, block), rows_of(seen, 3 * block, block), twin)
    to_twin[0].wait_recv()
    last.wait_recv()
    experts(0)
    share(0)
    for copy in shared:
        copy.wait_recv()

    def joined(chunk_index, part, start, size):
        own = made[pl.ds(chunk_index * chunk + part * block + start, size), :].astype(jnp.float32)
        return own + from_twin[pl.ds(chunk_index * 2 * block + part * block + start, size), :].astype(jnp.float32)

    made[block : 2 * block, :] = joined(0, 1, 0, block).astype(made.dtype)
    to_left = send(rows_of(made, block, half), rows_of(half_sums, 0, half), left)
    to_right = send(rows_of(made, block + half, half), rows_of(half_sums, half, half), right)
    for s in range(far - 1, 0, -1):
        base = s * chunk
        slot = (s - 1) * 2 * block
        to_left.wait_recv()
        if s == far - 1:
            made[base : base + half, :] = (
                joined(s, 0, 0, half) + half_sums[0:half, :].astype(jnp.float32)
            ).astype(made.dtype)
            made[base + half : base + block, :] = joined(s, 0, half, half).astype(made.dtype)
        else:
            arrived = sums[slot + 2 * block : slot + 3 * block, :].astype(jnp.float32)
            made[base : base + block, :] = (joined(s, 0, 0, block) + arrived).astype(made.dtype)
        to_left = send(rows_of(made, base, block), rows_of(sums, slot, block), left)
        to_right.wait_recv()
        if s == far - 1:
            made[base + block : base + block + half, :] = joined(s, 1, 0, half).astype(made.dtype)
            made[base + block + half : base + 2 * block, :] = (
                joined(s, 1, half, half) + half_sums[half:block, :].astype(jnp.float32)
            ).astype(made.dtype)
        else:
            arrived = sums[slot + 3 * block : slot + 4 * block, :].astype(jnp.float32)
            made[base + block : base + 2 * block, :] = (joined(s, 1, 0, block) + arrived).astype(made.dtype)
        to_right = send(rows_of(made, base + block, block), rows_of(sums, slot + block, block), right)
    to_left.wait_recv()
    to_right.wait_recv()
    out_ref[...] = (
        joined(0, 0, 0, block) + sums[0:block, :].astype(jnp.float32) + sums[block : 2 * block, :].astype(jnp.float32)
    )
    for copy in copies:
        copy.wait_send()


def expert_rings(block, w_gate, w_up, w_down, n_ep, snake):
    rows, wide = block.shape
    model, hidden_units = w_gate.shape[1], w_gate.shape[2]
    far = n_ep // 4
    assert far == 4 and w_gate.shape[0] == 1 and rows % 32 == 0
    n_copies = 3 + 3 * (far - 1) + 1 + far + 2 + 2 * (far - 1)
    bf16 = jnp.bfloat16
    return pl.pallas_call(
        functools.partial(ring_kernel, n_ep, snake),
        out_shape=jax.ShapeDtypeStruct((rows, model), jnp.float32),
        in_specs=[pl.BlockSpec(memory_space=pltpu.VMEM)] + [pl.BlockSpec(memory_space=pl.ANY)] * 3,
        out_specs=pl.BlockSpec(memory_space=pltpu.VMEM),
        scratch_shapes=[
            pltpu.VMEM((n_ep * rows, wide), bf16),
            pltpu.VMEM((n_ep * rows, model), bf16),
            pltpu.VMEM((n_ep // 2 * rows, model), bf16),
            pltpu.VMEM(((far - 1) * 2 * rows, model), bf16),
            pltpu.VMEM((rows, model), bf16),
            pltpu.VMEM((4 * rows, hidden_units), bf16),
            pltpu.VMEM((model, hidden_units), bf16),
            pltpu.VMEM((model, hidden_units), bf16),
            pltpu.VMEM((hidden_units, model), bf16),
            pltpu.SemaphoreType.DMA((n_copies,)),
            pltpu.SemaphoreType.DMA((n_copies,)),
            pltpu.SemaphoreType.DMA((3,)),
        ],
        compiler_params=pltpu.CompilerParams(
            collective_id=0, has_side_effects=True, vmem_limit_bytes=48 * 1024 * 1024
        ),
        cost_estimate=pl.CostEstimate(
            flops=6 * n_ep * rows * model * hidden_units,
            bytes_accessed=6 * model * hidden_units,
            transcendentals=0,
        ),
        name="expert_rings",
    )(block, w_gate, w_up, w_down)


def shards(
    hidden_in,
    queries,
    new_latents,
    cache,
    prefill_pool,
    requests,
    context_len,
    picks,
    w_uv,
    w_out,
    norm_gain,
    router,
    w_gate,
    w_up,
    w_down,
):
    n_ep = lax.axis_size("ep")
    steps, rows, share = hidden_in.shape
    heads, width = queries.shape[2], queries.shape[3]
    res, pool, top = cache.shape[0], prefill_pool.shape[0], picks.shape[2]
    experts, model = router.shape[1], router.shape[0]
    bf16 = jnp.bfloat16

    member = jnp.any(picks[..., None] == jnp.arange(experts), axis=2).astype(bf16)

    notes = 3 + experts
    extra = -(-(share + notes) // width)
    note = jnp.concatenate(
        [
            jnp.broadcast_to(jnp.stack([requests % pool + 1, context_len[res:] // 128, context_len[res:] % 128], axis=1).astype(bf16), (steps, pool, 3)),
            member[:, res:],
            jnp.zeros((steps, pool, extra * width - share - notes), bf16),
        ],
        axis=2,
    )
    riders = jnp.concatenate([hidden_in[:, res:], note], axis=2).reshape(steps, pool, extra, width)
    packed = jnp.concatenate([queries[:, res:], new_latents[:, res:, None, :], riders], axis=2)
    to_owner = (jnp.arange(n_ep)[:, None] == (requests // pool)[None, :]).astype(bf16)
    outgoing = jnp.einsum("dk,tkhc->dthc", to_owner, packed, preferred_element_type=jnp.float32).astype(bf16)
    arrived = lax.all_to_all(outgoing, "ep", split_axis=0, concat_axis=0, tiled=True)
    slot_asked = arrived[:, 0, heads + 1 + share // width, share % width].astype(jnp.int32)
    from_asker = (slot_asked[None, :] == 1 + jnp.arange(pool)[:, None]).astype(bf16)
    taken = jnp.einsum("pe,ethc->tphc", from_asker, arrived, preferred_element_type=jnp.float32).astype(bf16)
    moved_queries = taken[:, :, :heads]
    moved_latents = taken[:, :, heads]
    riders = taken[:, :, heads + 1 :].reshape(steps, pool, extra * width)
    moved_hidden = riders[:, :, :share]
    ctx_parts = riders[0, :, share + 1 : share + 3].astype(jnp.int32)
    moved_ctx = ctx_parts[:, 0] * 128 + ctx_parts[:, 1]
    moved_member = riders[:, :, share + 3 : share + 3 + experts]

    if lax.axis_size("tp") > 1:
        cache = lax.all_gather(cache, "tp", axis=1, tiled=True)
        prefill_pool = lax.all_gather(prefill_pool, "tp", axis=1, tiled=True)
    latent = jnp.concatenate(
        [
            attend_rows(queries[:, :res], new_latents[:, :res], cache, context_len[:res]),
            attend_rows(moved_queries, moved_latents, prefill_pool, moved_ctx),
        ],
        axis=1,
    )
    values = jnp.einsum("trhc,hcv->trhv", latent, w_uv, preferred_element_type=jnp.float32).astype(bf16)
    partial_value = jnp.einsum("trhv,hvd->trd", values, w_out, preferred_element_type=jnp.float32)
    hidden_rows = jnp.concatenate([hidden_in[:, :res], moved_hidden], axis=1).astype(jnp.float32)
    tp = lax.axis_index("tp")
    if lax.axis_size("tp") > 1:
        column = tp * share
        placed = lax.dynamic_update_slice_in_dim(jnp.zeros_like(partial_value), hidden_rows, column, 2)
        hidden = lax.psum(partial_value + placed, "tp")
        own_cols = lax.dynamic_slice_in_dim(hidden, column, share, 2)
    else:
        hidden = partial_value + hidden_rows
        own_cols = hidden
    scale = lax.rsqrt(jnp.mean(hidden * hidden, axis=-1, keepdims=True) + NORM_EPS)
    normed = (hidden * scale * norm_gain).astype(bf16)

    affinity = jax.nn.sigmoid(jnp.einsum("trd,de->tre", normed, router, preferred_element_type=jnp.float32))
    members = jnp.concatenate([member[:, :res], moved_member], axis=1)
    chosen = jnp.where(members > 0, affinity, 0.0)
    gates = chosen / jnp.sum(chosen, axis=-1, keepdims=True) * ROUTE_SCALE
    coarse = gates.astype(bf16)
    fine = (gates - coarse.astype(jnp.float32)).astype(bf16)
    blank = jnp.zeros((steps, rows, 128 - 2 * experts), bf16)
    block = jnp.concatenate([normed, coarse, fine, blank], axis=2).reshape(steps * rows, model + 128)
    mixed = expert_rings(block, w_gate, w_up, w_down, n_ep, lax.axis_size("tp") == 1)
    mixed = mixed.reshape(steps, rows, model)
    if lax.axis_size("tp") > 1:
        mixed = lax.psum_scatter(mixed, "tp", scatter_dimension=2, tiled=True)
    done = (own_cols + mixed).astype(bf16)

    going_back = jnp.einsum("pe,tpd->etd", from_asker, done[:, res:], preferred_element_type=jnp.float32).astype(bf16)
    back = lax.all_to_all(going_back, "ep", split_axis=0, concat_axis=0, tiled=True)
    own_again = jnp.einsum("ek,etd->tkd", to_owner, back, preferred_element_type=jnp.float32).astype(bf16)
    return jnp.concatenate([done[:, :res], own_again], axis=1)


def solution(mesh):
    in_specs = (
        P(None, ("group", "ep"), "tp"),
        P(None, ("group", "ep"), "tp", None),
        P(None, ("group", "ep"), None),
        P(("group", "ep"), "tp", None),
        P(("group", "ep"), "tp", None),
        P(("group", "ep")),
        P(("group", "ep")),
        P(None, ("group", "ep"), None),
        P("tp", None, None),
        P("tp", None, None),
        P(),
        P(),
        P("ep", None, "tp"),
        P("ep", None, "tp"),
        P("ep", "tp", None),
    )
    out_specs = P(None, ("group", "ep"), "tp")
    return jax.shard_map(shards, mesh=mesh, in_specs=in_specs, out_specs=out_specs, check_vma=False)
```

```python
import functools

import jax
import jax.numpy as jnp
from jax import lax
from jax.experimental import pallas as pl
from jax.experimental.pallas import tpu as pltpu
from jax.sharding import PartitionSpec as P

LAT = 512

SOFT_SCALE = 192.0 ** (-0.5)
ROUTE_SCALE = 2.5
NORM_EPS = 1e-06
NEG_FILL = -1e30


def attend_rows(queries, new_latents, rows_cache, context_len):
    steps = queries.shape[0]
    fresh = (
        jnp.einsum("trhc,urc->trhu", queries, new_latents, preferred_element_type=jnp.float32)
        * SOFT_SCALE
    )
    live = jnp.arange(steps)[None, :] <= jnp.arange(steps)[:, None]
    fresh = jnp.where(live[:, None, None, :], fresh, NEG_FILL)
    scores = (
        jnp.einsum("trhc,rjc->trhj", queries, rows_cache, preferred_element_type=jnp.float32)
        * SOFT_SCALE
    )
    valid = jnp.arange(rows_cache.shape[1])[None, :] < context_len[:, None]
    scores = jnp.where(valid[None, :, None, :], scores, NEG_FILL)
    peak = jnp.maximum(jnp.max(fresh, axis=-1), jnp.max(scores, axis=-1))
    fresh_weights = jnp.exp(fresh - peak[..., None])
    weights = jnp.exp(scores - peak[..., None])
    total = jnp.sum(fresh_weights, axis=-1) + jnp.sum(weights, axis=-1)
    acc = jnp.einsum(
        "trhj,rjc->trhc",
        weights.astype(jnp.bfloat16),
        rows_cache[:, :, :LAT],
        preferred_element_type=jnp.float32,
    )
    for u in range(steps):
        acc = acc + fresh_weights[..., u, None] * new_latents[u, None, :, None, :LAT].astype(jnp.float32)
    return (acc / total[..., None]).astype(jnp.bfloat16)


def ring_kernel(
    n_ep, snake, moved, block_ref, hidden_ref, gate_hbm, up_hbm, down_hbm, out_ref,
    seen, made, from_twin, sums, half_sums, active, w_gate, w_up, w_down,
    send_sem, recv_sem, load_sem,
):
    chips = n_ep // 2
    me = lax.axis_index("ep")
    chip, core = me // 2, me % 2
    if snake:
        place = jnp.where(chip % 2 == 0, chip // 2, chips - 1 - chip // 2)
        at = lambda p: jnp.where(p < chips // 2, 2 * p, 2 * (chips - 1 - p) + 1)
    else:
        place = chip
        at = lambda p: p
    right = at((place + 1) % chips) * 2 + core
    left = at((place + chips - 1) % chips) * 2 + core
    twin = chip * 2 + 1 - core
    block, model = out_ref.shape
    half = block // 2
    chunk = 4 * block
    far = chips // 2

    barrier = pltpu.get_barrier_semaphore()
    for other in (left, right, twin):
        pl.semaphore_signal(barrier, inc=1, device_id={"ep": other}, device_id_type=pl.DeviceIdType.MESH)
    pl.semaphore_wait(barrier, 3)

    loads = [
        pltpu.make_async_copy(hbm.at[0], vmem, load_sem.at[i])
        for i, (hbm, vmem) in enumerate(((gate_hbm, w_gate), (up_hbm, w_up), (down_hbm, w_down)))
    ]
    copies = []

    def send(src, dst, to):
        k = len(copies)
        copy = pltpu.make_async_remote_copy(
            src_ref=src, dst_ref=dst, send_sem=send_sem.at[k], recv_sem=recv_sem.at[k],
            device_id={"ep": to}, device_id_type=pl.DeviceIdType.MESH,
        )
        copy.start()
        copies.append(copy)
        return copy

    def rows_of(ref, start, size):
        return ref.at[pl.ds(start, size), :]

    to_right = send(block_ref, rows_of(seen, chunk, block), right)
    to_left = send(block_ref, rows_of(seen, chunk + block, block), left)
    to_twin = [send(block_ref, rows_of(seen, 2 * block, block), twin)]
    for load in loads:
        load.start()
    seen[0:block, :] = block_ref[...]

    def experts(index):
        base = index * chunk
        f_tile = min(256, w_gate.shape[1])
        d_tile = 512 if model % 512 == 0 else 128

        @pl.loop(0, w_gate.shape[1] // f_tile)
        def _(i):
            columns = pl.ds(pl.multiple_of(i * f_tile, f_tile), f_tile)
            rows = seen[base : base + chunk, :model]
            gate = jnp.dot(rows, w_gate[:, columns], preferred_element_type=jnp.float32)
            upper = jnp.dot(rows, w_up[:, columns], preferred_element_type=jnp.float32)
            active[:, columns] = (gate / (1.0 + jnp.exp(-gate)) * upper).astype(active.dtype)

        carried = seen[base : base + chunk, model:].astype(jnp.float32)
        lane = lax.broadcasted_iota(jnp.int32, carried.shape, 1)
        weight = jnp.sum(jnp.where((lane == me) | (lane == me + n_ep), carried, 0.0), axis=1, keepdims=True)

        @pl.loop(0, model // d_tile)
        def _(i):
            columns = pl.ds(pl.multiple_of(i * d_tile, d_tile), d_tile)
            produced = jnp.dot(active[...], w_down[:, columns], preferred_element_type=jnp.float32)
            made[base : base + chunk, columns] = (produced * weight).astype(made.dtype)

    shared = []

    def share(index):
        shared.append(
            send(rows_of(made, index * chunk + 2 * block, 2 * block), rows_of(from_twin, index * 2 * block, 2 * block), twin)
        )

    for s in range(1, far):
        base = s * chunk
        to_right.wait_recv()
        if s < far - 1:
            to_right = send(rows_of(seen, base, block), rows_of(seen, base + chunk, block), right)
        else:
            to_right = send(rows_of(seen, base, half), rows_of(seen, block, half), right)
        to_left.wait_recv()
        if s < far - 1:
            to_left = send(rows_of(seen, base + block, block), rows_of(seen, base + chunk + block, block), left)
        else:
            to_left = send(rows_of(seen, base + block + half, half), rows_of(seen, block + half, half), left)
        both = send(rows_of(seen, base, 2 * block), rows_of(seen, base + 2 * block, 2 * block), twin)
        if s == 1:
            for load in loads:
                load.wait()
        both.wait_recv()
        experts(s)
    to_right.wait_recv()
    to_left.wait_recv()
    last = send(rows_of(seen, block, block), rows_of(seen, 3 * block, block), twin)
    to_twin[0].wait_recv()
    last.wait_recv()
    experts(0)

    blocks = [(chunk_index, part) for chunk_index in range(far) for part in range(4)]
    tail = block - 2 * moved

    def held_by(chunk_index, part):
        steps_away = far if part % 2 else 0
        if chunk_index:
            steps_away = chunk_index if part % 2 else -chunk_index
        return at((place + steps_away + chips) % chips) * 2 + (core if part < 2 else 1 - core)

    def lower(ref, index, columns):
        return ref[index * block + tail : (index + 1) * block, columns].astype(jnp.float32)

    carried = jnp.concatenate(
        [lower(seen, i, slice(model, None))[moved:] for i in range(len(blocks))], axis=0
    )
    lane = lax.broadcasted_iota(jnp.int32, carried.shape, 1)
    asker = jnp.sum(jnp.where(lane == 2 * n_ep, carried, 0.0), axis=1, keepdims=True)
    asker_row = jnp.sum(jnp.where(lane == 2 * n_ep + 1, carried, 0.0), axis=1, keepdims=True)
    count = len(blocks) * moved
    spot = lax.broadcasted_iota(jnp.int32, (1, count), 1)
    holder = jnp.zeros((1, count), jnp.int32)
    for i, (chunk_index, part) in enumerate(blocks):
        holder = jnp.where(spot // moved == i, held_by(chunk_index, part), holder)
    wanted = (holder * moved + spot % moved).astype(jnp.float32)
    order = jnp.where(asker * moved + asker_row == wanted, 1.0, 0.0).astype(made.dtype)
    d_tile = 512 if model % 512 == 0 else 128

    @pl.loop(0, model // d_tile)
    def _(i):
        columns = pl.ds(pl.multiple_of(i * d_tile, d_tile), d_tile)
        ends = [lower(made, n, columns) for n in range(len(blocks))]
        outputs = [end[moved:] for end in ends]
        outputs[0] = outputs[0] + hidden_ref[:, columns]
        outputs = jnp.concatenate(outputs, axis=0).astype(made.dtype)
        placed = lax.dot_general(
            order, outputs, (((0,), (0,)), ((), ())), preferred_element_type=jnp.float32
        )
        for n, end in enumerate(ends):
            mixed_rows = jnp.concatenate([end[:moved], placed[n * moved : (n + 1) * moved]], axis=0)
            made[n * block + tail : (n + 1) * block, columns] = mixed_rows.astype(made.dtype)

    share(0)
    for s in range(far - 1, 0, -1):
        share(s)
    shared[0].wait_recv()

    def joined(chunk_index, part, start, size):
        own = made[pl.ds(chunk_index * chunk + part * block + start, size), :].astype(jnp.float32)
        return own + from_twin[pl.ds(chunk_index * 2 * block + part * block + start, size), :].astype(jnp.float32)

    made[block : 2 * block, :] = joined(0, 1, 0, block).astype(made.dtype)
    to_left = send(rows_of(made, block, half), rows_of(half_sums, 0, half), left)
    to_right = send(rows_of(made, block + half, half), rows_of(half_sums, half, half), right)
    for s in range(far - 1, 0, -1):
        base = s * chunk
        slot = (s - 1) * 2 * block
        shared[far - s].wait_recv()
        to_left.wait_recv()
        if s == far - 1:
            made[base : base + half, :] = (
                joined(s, 0, 0, half) + half_sums[0:half, :].astype(jnp.float32)
            ).astype(made.dtype)
            made[base + half : base + block, :] = joined(s, 0, half, half).astype(made.dtype)
        else:
            arrived = sums[slot + 2 * block : slot + 3 * block, :].astype(jnp.float32)
            made[base : base + block, :] = (joined(s, 0, 0, block) + arrived).astype(made.dtype)
        to_left = send(rows_of(made, base, block), rows_of(sums, slot, block), left)
        to_right.wait_recv()
        if s == far - 1:
            made[base + block : base + block + half, :] = joined(s, 1, 0, half).astype(made.dtype)
            made[base + block + half : base + 2 * block, :] = (
                joined(s, 1, half, half) + half_sums[half:block, :].astype(jnp.float32)
            ).astype(made.dtype)
        else:
            arrived = sums[slot + 3 * block : slot + 4 * block, :].astype(jnp.float32)
            made[base + block : base + 2 * block, :] = (joined(s, 1, 0, block) + arrived).astype(made.dtype)
        to_right = send(rows_of(made, base + block, block), rows_of(sums, slot + block, block), right)
    to_left.wait_recv()
    to_right.wait_recv()
    out_ref[...] = (
        joined(0, 0, 0, block) + sums[0:block, :].astype(jnp.float32) + sums[block : 2 * block, :].astype(jnp.float32)
    )
    for copy in copies:
        copy.wait_send()


def expert_rings(block, hidden, w_gate, w_up, w_down, n_ep, snake):
    rows, wide = block.shape
    model, hidden_units = w_gate.shape[1], w_gate.shape[2]
    far = n_ep // 4
    assert far == 4 and w_gate.shape[0] == 1 and rows % 32 == 0
    n_copies = 3 + 3 * (far - 1) + 1 + far + 2 + 2 * (far - 1)
    bf16 = jnp.bfloat16
    return pl.pallas_call(
        functools.partial(ring_kernel, n_ep, snake, hidden.shape[0]),
        out_shape=jax.ShapeDtypeStruct((rows, model), jnp.float32),
        in_specs=[pl.BlockSpec(memory_space=pltpu.VMEM)] * 2 + [pl.BlockSpec(memory_space=pl.ANY)] * 3,
        out_specs=pl.BlockSpec(memory_space=pltpu.VMEM),
        scratch_shapes=[
            pltpu.VMEM((n_ep * rows, wide), bf16),
            pltpu.VMEM((n_ep * rows, model), bf16),
            pltpu.VMEM((n_ep // 2 * rows, model), bf16),
            pltpu.VMEM(((far - 1) * 2 * rows, model), bf16),
            pltpu.VMEM((rows, model), bf16),
            pltpu.VMEM((4 * rows, hidden_units), bf16),
            pltpu.VMEM((model, hidden_units), bf16),
            pltpu.VMEM((model, hidden_units), bf16),
            pltpu.VMEM((hidden_units, model), bf16),
            pltpu.SemaphoreType.DMA((n_copies,)),
            pltpu.SemaphoreType.DMA((n_copies,)),
            pltpu.SemaphoreType.DMA((3,)),
        ],
        compiler_params=pltpu.CompilerParams(
            collective_id=0, has_side_effects=True, vmem_limit_bytes=48 * 1024 * 1024
        ),
        cost_estimate=pl.CostEstimate(
            flops=6 * n_ep * rows * model * hidden_units,
            bytes_accessed=6 * model * hidden_units,
            transcendentals=0,
        ),
        name="expert_rings",
    )(block, hidden, w_gate, w_up, w_down)


def shards(
    hidden_in,
    queries,
    new_latents,
    cache,
    prefill_pool,
    requests,
    context_len,
    picks,
    w_uv,
    w_out,
    norm_gain,
    router,
    w_gate,
    w_up,
    w_down,
):
    n_ep = lax.axis_size("ep")
    steps, rows, share = hidden_in.shape
    heads, width = queries.shape[2], queries.shape[3]
    res, pool, top = cache.shape[0], prefill_pool.shape[0], picks.shape[2]
    experts, model = router.shape[1], router.shape[0]
    bf16 = jnp.bfloat16

    member = jnp.any(picks[..., None] == jnp.arange(experts), axis=2).astype(bf16)

    notes = 4 + experts
    extra = -(-(share + notes) // width)
    note = jnp.concatenate(
        [
            jnp.broadcast_to(
                jnp.stack(
                    [requests % pool + 1, context_len[res:] // 128, context_len[res:] % 128, jnp.arange(pool)],
                    axis=1,
                ).astype(bf16),
                (steps, pool, 4),
            ),
            member[:, res:],
            jnp.zeros((steps, pool, extra * width - share - notes), bf16),
        ],
        axis=2,
    )
    riders = jnp.concatenate([hidden_in[:, res:], note], axis=2).reshape(steps, pool, extra, width)
    packed = jnp.concatenate([queries[:, res:], new_latents[:, res:, None, :], riders], axis=2)
    to_owner = (jnp.arange(n_ep)[:, None] == (requests // pool)[None, :]).astype(bf16)
    outgoing = jnp.einsum("dk,tkhc->dthc", to_owner, packed, preferred_element_type=jnp.float32).astype(bf16)
    arrived = lax.all_to_all(outgoing, "ep", split_axis=0, concat_axis=0, tiled=True)
    slot_asked = arrived[:, 0, heads + 1 + share // width, share % width].astype(jnp.int32)
    from_asker = (slot_asked[None, :] == 1 + jnp.arange(pool)[:, None]).astype(bf16)
    taken = jnp.einsum("pe,ethc->tphc", from_asker, arrived, preferred_element_type=jnp.float32).astype(bf16)
    moved_queries = taken[:, :, :heads]
    moved_latents = taken[:, :, heads]
    riders = taken[:, :, heads + 1 :].reshape(steps, pool, extra * width)
    moved_hidden = riders[:, :, :share]
    ctx_parts = riders[0, :, share + 1 : share + 3].astype(jnp.int32)
    moved_ctx = ctx_parts[:, 0] * 128 + ctx_parts[:, 1]
    moved_member = riders[:, :, share + 4 : share + 4 + experts]
    asker_row = riders[:, :, share + 3] + (pool * jnp.arange(steps)[:, None]).astype(bf16)
    asker = jnp.broadcast_to(
        jnp.sum(from_asker * jnp.arange(n_ep).astype(bf16), axis=1), (steps, pool)
    )

    if lax.axis_size("tp") > 1:
        cache = lax.all_gather(cache, "tp", axis=1, tiled=True)
        prefill_pool = lax.all_gather(prefill_pool, "tp", axis=1, tiled=True)
    latent = jnp.concatenate(
        [
            attend_rows(queries[:, :res], new_latents[:, :res], cache, context_len[:res]),
            attend_rows(moved_queries, moved_latents, prefill_pool, moved_ctx),
        ],
        axis=1,
    )
    values = jnp.einsum("trhc,hcv->trhv", latent, w_uv, preferred_element_type=jnp.float32).astype(bf16)
    partial_value = jnp.einsum("trhv,hvd->trd", values, w_out, preferred_element_type=jnp.float32)
    hidden_rows = jnp.concatenate([hidden_in[:, :res], moved_hidden], axis=1).astype(jnp.float32)
    tp = lax.axis_index("tp")
    if lax.axis_size("tp") > 1:
        column = tp * share
        placed = lax.dynamic_update_slice_in_dim(jnp.zeros_like(partial_value), hidden_rows, column, 2)
        hidden = lax.psum(partial_value + placed, "tp")
        own_cols = lax.dynamic_slice_in_dim(hidden, column, share, 2)
    else:
        hidden = partial_value + hidden_rows
        own_cols = hidden
    scale = lax.rsqrt(jnp.mean(hidden * hidden, axis=-1, keepdims=True) + NORM_EPS)
    normed = (hidden * scale * norm_gain).astype(bf16)

    affinity = jax.nn.sigmoid(jnp.einsum("trd,de->tre", normed, router, preferred_element_type=jnp.float32))
    members = jnp.concatenate([member[:, :res], moved_member], axis=1)
    chosen = jnp.where(members > 0, affinity, 0.0)
    gates = chosen / jnp.sum(chosen, axis=-1, keepdims=True) * ROUTE_SCALE
    coarse = gates.astype(bf16)
    fine = (gates - coarse.astype(jnp.float32)).astype(bf16)
    address = jnp.stack([asker, asker_row], axis=-1)
    address = jnp.concatenate([jnp.zeros((steps, res, 2), bf16), address], axis=1)
    blank = jnp.zeros((steps, rows, 126 - 2 * experts), bf16)
    block = jnp.concatenate([normed, coarse, fine, address, blank], axis=2)
    wide = model + 128
    block = jnp.concatenate(
        [block[:, :res].reshape(steps * res, wide), block[:, res:].reshape(steps * pool, wide)], axis=0
    )
    moved_hidden = hidden[:, res:].reshape(steps * pool, model)
    if lax.axis_size("tp") > 1:
        moved_hidden = jnp.where(tp == 0, moved_hidden, 0.0)
    mixed = expert_rings(block, moved_hidden, w_gate, w_up, w_down, n_ep, lax.axis_size("tp") == 1)
    mixed = jnp.concatenate(
        [mixed[: steps * res].reshape(steps, res, model), mixed[steps * res :].reshape(steps, pool, model)], axis=1
    )
    if lax.axis_size("tp") > 1:
        mixed = lax.psum_scatter(mixed, "tp", scatter_dimension=2, tiled=True)
    resident = jnp.arange(rows)[None, :, None] < res
    return (jnp.where(resident, own_cols, 0.0) + mixed).astype(bf16)


def solution(mesh):
    in_specs = (
        P(None, ("group", "ep"), "tp"),
        P(None, ("group", "ep"), "tp", None),
        P(None, ("group", "ep"), None),
        P(("group", "ep"), "tp", None),
        P(("group", "ep"), "tp", None),
        P(("group", "ep")),
        P(("group", "ep")),
        P(None, ("group", "ep"), None),
        P("tp", None, None),
        P("tp", None, None),
        P(),
        P(),
        P("ep", None, "tp"),
        P("ep", None, "tp"),
        P("ep", "tp", None),
    )
    out_specs = P(None, ("group", "ep"), "tp")
    return jax.shard_map(shards, mesh=mesh, in_specs=in_specs, out_specs=out_specs, check_vma=False)
```

```python
import functools

import jax
import jax.numpy as jnp
from jax import lax
from jax.experimental import pallas as pl
from jax.experimental.pallas import tpu as pltpu
from jax.sharding import PartitionSpec as P

LAT = 512

SOFT_SCALE = 192.0 ** (-0.5)
ROUTE_SCALE = 2.5
NORM_EPS = 1e-06
NEG_FILL = -1e30


def attend_rows(queries, new_latents, rows_cache, context_len):
    steps = queries.shape[0]
    fresh = (
        jnp.einsum("trhc,urc->trhu", queries, new_latents, preferred_element_type=jnp.float32)
        * SOFT_SCALE
    )
    live = jnp.arange(steps)[None, :] <= jnp.arange(steps)[:, None]
    fresh = jnp.where(live[:, None, None, :], fresh, NEG_FILL)
    scores = (
        jnp.einsum("trhc,rjc->trhj", queries, rows_cache, preferred_element_type=jnp.float32)
        * SOFT_SCALE
    )
    valid = jnp.arange(rows_cache.shape[1])[None, :] < context_len[:, None]
    scores = jnp.where(valid[None, :, None, :], scores, NEG_FILL)
    peak = jnp.maximum(jnp.max(fresh, axis=-1), jnp.max(scores, axis=-1))
    fresh_weights = jnp.exp(fresh - peak[..., None])
    weights = jnp.exp(scores - peak[..., None])
    total = jnp.sum(fresh_weights, axis=-1) + jnp.sum(weights, axis=-1)
    acc = jnp.einsum(
        "trhj,rjc->trhc",
        weights.astype(jnp.bfloat16),
        rows_cache[:, :, :LAT],
        preferred_element_type=jnp.float32,
    )
    for u in range(steps):
        acc = acc + fresh_weights[..., u, None] * new_latents[u, None, :, None, :LAT].astype(jnp.float32)
    return (acc / total[..., None]).astype(jnp.bfloat16)


def ring_kernel(
    n_ep, snake, moved, block_ref, hidden_ref, gate_hbm, up_hbm, down_hbm, out_ref,
    seen, made, from_twin, sums, half_sums, active, w_gate, w_up, w_down,
    send_sem, recv_sem, load_sem,
):
    chips = n_ep // 2
    me = lax.axis_index("ep")
    chip, core = me // 2, me % 2
    if snake:
        place = jnp.where(chip % 2 == 0, chip // 2, chips - 1 - chip // 2)
        at = lambda p: jnp.where(p < chips // 2, 2 * p, 2 * (chips - 1 - p) + 1)
    else:
        place = chip
        at = lambda p: p
    right = at((place + 1) % chips) * 2 + core
    left = at((place + chips - 1) % chips) * 2 + core
    twin = chip * 2 + 1 - core
    block, model = out_ref.shape
    half = block // 2
    chunk = 4 * block
    far = chips // 2

    barrier = pltpu.get_barrier_semaphore()
    for other in (left, right, twin):
        pl.semaphore_signal(barrier, inc=1, device_id={"ep": other}, device_id_type=pl.DeviceIdType.MESH)
    pl.semaphore_wait(barrier, 3)

    loads = [
        pltpu.make_async_copy(hbm.at[0], vmem, load_sem.at[i])
        for i, (hbm, vmem) in enumerate(((gate_hbm, w_gate), (up_hbm, w_up), (down_hbm, w_down)))
    ]
    copies = []

    def send(src, dst, to):
        k = len(copies)
        copy = pltpu.make_async_remote_copy(
            src_ref=src, dst_ref=dst, send_sem=send_sem.at[k], recv_sem=recv_sem.at[k],
            device_id={"ep": to}, device_id_type=pl.DeviceIdType.MESH,
        )
        copy.start()
        copies.append(copy)
        return copy

    def rows_of(ref, start, size):
        return ref.at[pl.ds(start, size), :]

    to_right = send(block_ref, rows_of(seen, chunk, block), right)
    to_left = send(block_ref, rows_of(seen, chunk + block, block), left)
    to_twin = [send(block_ref, rows_of(seen, 2 * block, block), twin)]
    for load in loads:
        load.start()
    seen[0:block, :] = block_ref[...]

    def experts(index):
        base = index * chunk
        f_tile = min(512, w_gate.shape[1])
        d_tile = 512 if model % 512 == 0 else 128

        @pl.loop(0, w_gate.shape[1] // f_tile)
        def _(i):
            columns = pl.ds(pl.multiple_of(i * f_tile, f_tile), f_tile)
            rows = seen[base : base + chunk, :model]
            gate = jnp.dot(rows, w_gate[:, columns], preferred_element_type=jnp.float32)
            upper = jnp.dot(rows, w_up[:, columns], preferred_element_type=jnp.float32)
            active[:, columns] = (gate / (1.0 + jnp.exp(-gate)) * upper).astype(active.dtype)

        carried = seen[base : base + chunk, model:].astype(jnp.float32)
        lane = lax.broadcasted_iota(jnp.int32, carried.shape, 1)
        weight = jnp.sum(jnp.where((lane == me) | (lane == me + n_ep), carried, 0.0), axis=1, keepdims=True)

        @pl.loop(0, model // d_tile)
        def _(i):
            columns = pl.ds(pl.multiple_of(i * d_tile, d_tile), d_tile)
            produced = jnp.dot(active[...], w_down[:, columns], preferred_element_type=jnp.float32)
            made[base : base + chunk, columns] = (produced * weight).astype(made.dtype)

    shared = []

    def share(index):
        shared.append(
            send(rows_of(made, index * chunk + 2 * block, 2 * block), rows_of(from_twin, index * 2 * block, 2 * block), twin)
        )

    for s in range(1, far):
        base = s * chunk
        to_right.wait_recv()
        if s < far - 1:
            to_right = send(rows_of(seen, base, block), rows_of(seen, base + chunk, block), right)
        else:
            to_right = send(rows_of(seen, base, half), rows_of(seen, block, half), right)
        to_left.wait_recv()
        if s < far - 1:
            to_left = send(rows_of(seen, base + block, block), rows_of(seen, base + chunk + block, block), left)
        else:
            to_left = send(rows_of(seen, base + block + half, half), rows_of(seen, block + half, half), left)
        both = send(rows_of(seen, base, 2 * block), rows_of(seen, base + 2 * block, 2 * block), twin)
        if s == 1:
            for load in loads:
                load.wait()
        both.wait_recv()
        experts(s)
    to_right.wait_recv()
    to_left.wait_recv()
    last = send(rows_of(seen, block, block), rows_of(seen, 3 * block, block), twin)
    to_twin[0].wait_recv()
    last.wait_recv()
    experts(0)

    blocks = [(chunk_index, part) for chunk_index in range(far) for part in range(4)]
    tail = block - 2 * moved

    def held_by(chunk_index, part):
        steps_away = far if part % 2 else 0
        if chunk_index:
            steps_away = chunk_index if part % 2 else -chunk_index
        return at((place + steps_away + chips) % chips) * 2 + (core if part < 2 else 1 - core)

    def lower(ref, index, columns):
        return ref[index * block + tail : (index + 1) * block, columns].astype(jnp.float32)

    carried = jnp.concatenate(
        [lower(seen, i, slice(model, None))[moved:] for i in range(len(blocks))], axis=0
    )
    lane = lax.broadcasted_iota(jnp.int32, carried.shape, 1)
    asker = jnp.sum(jnp.where(lane == 2 * n_ep, carried, 0.0), axis=1, keepdims=True)
    asker_row = jnp.sum(jnp.where(lane == 2 * n_ep + 1, carried, 0.0), axis=1, keepdims=True)
    count = len(blocks) * moved
    spot = lax.broadcasted_iota(jnp.int32, (1, count), 1)
    holder = jnp.zeros((1, count), jnp.int32)
    for i, (chunk_index, part) in enumerate(blocks):
        holder = jnp.where(spot // moved == i, held_by(chunk_index, part), holder)
    wanted = (holder * moved + spot % moved).astype(jnp.float32)
    order = jnp.where(asker * moved + asker_row == wanted, 1.0, 0.0).astype(made.dtype)
    d_tile = 512 if model % 512 == 0 else 128

    @pl.loop(0, model // d_tile)
    def _(i):
        columns = pl.ds(pl.multiple_of(i * d_tile, d_tile), d_tile)
        ends = [lower(made, n, columns) for n in range(len(blocks))]
        outputs = [end[moved:] for end in ends]
        outputs[0] = outputs[0] + hidden_ref[:, columns]
        outputs = jnp.concatenate(outputs, axis=0).astype(made.dtype)
        placed = lax.dot_general(
            order, outputs, (((0,), (0,)), ((), ())), preferred_element_type=jnp.float32
        )
        for n, end in enumerate(ends):
            mixed_rows = jnp.concatenate([end[:moved], placed[n * moved : (n + 1) * moved]], axis=0)
            made[n * block + tail : (n + 1) * block, columns] = mixed_rows.astype(made.dtype)

    share(0)
    for s in range(far - 1, 0, -1):
        share(s)
    shared[0].wait_recv()

    def joined(chunk_index, part, start, size):
        own = made[pl.ds(chunk_index * chunk + part * block + start, size), :].astype(jnp.float32)
        return own + from_twin[pl.ds(chunk_index * 2 * block + part * block + start, size), :].astype(jnp.float32)

    made[block : 2 * block, :] = joined(0, 1, 0, block).astype(made.dtype)
    to_left = send(rows_of(made, block, half), rows_of(half_sums, 0, half), left)
    to_right = send(rows_of(made, block + half, half), rows_of(half_sums, half, half), right)
    for s in range(far - 1, 0, -1):
        base = s * chunk
        slot = (s - 1) * 2 * block
        shared[far - s].wait_recv()
        to_left.wait_recv()
        if s == far - 1:
            made[base : base + half, :] = (
                joined(s, 0, 0, half) + half_sums[0:half, :].astype(jnp.float32)
            ).astype(made.dtype)
            made[base + half : base + block, :] = joined(s, 0, half, half).astype(made.dtype)
        else:
            arrived = sums[slot + 2 * block : slot + 3 * block, :].astype(jnp.float32)
            made[base : base + block, :] = (joined(s, 0, 0, block) + arrived).astype(made.dtype)
        to_left = send(rows_of(made, base, block), rows_of(sums, slot, block), left)
        to_right.wait_recv()
        if s == far - 1:
            made[base + block : base + block + half, :] = joined(s, 1, 0, half).astype(made.dtype)
            made[base + block + half : base + 2 * block, :] = (
                joined(s, 1, half, half) + half_sums[half:block, :].astype(jnp.float32)
            ).astype(made.dtype)
        else:
            arrived = sums[slot + 3 * block : slot + 4 * block, :].astype(jnp.float32)
            made[base + block : base + 2 * block, :] = (joined(s, 1, 0, block) + arrived).astype(made.dtype)
        to_right = send(rows_of(made, base + block, block), rows_of(sums, slot + block, block), right)
    to_left.wait_recv()
    to_right.wait_recv()
    out_ref[...] = (
        joined(0, 0, 0, block) + sums[0:block, :].astype(jnp.float32) + sums[block : 2 * block, :].astype(jnp.float32)
    )
    for copy in copies:
        copy.wait_send()


def expert_rings(block, hidden, w_gate, w_up, w_down, n_ep, snake):
    rows, wide = block.shape
    model, hidden_units = w_gate.shape[1], w_gate.shape[2]
    far = n_ep // 4
    assert far == 4 and w_gate.shape[0] == 1 and rows % 32 == 0
    n_copies = 3 + 3 * (far - 1) + 1 + far + 2 + 2 * (far - 1)
    bf16 = jnp.bfloat16
    return pl.pallas_call(
        functools.partial(ring_kernel, n_ep, snake, hidden.shape[0]),
        out_shape=jax.ShapeDtypeStruct((rows, model), jnp.float32),
        in_specs=[pl.BlockSpec(memory_space=pltpu.VMEM)] * 2 + [pl.BlockSpec(memory_space=pl.ANY)] * 3,
        out_specs=pl.BlockSpec(memory_space=pltpu.VMEM),
        scratch_shapes=[
            pltpu.VMEM((n_ep * rows, wide), bf16),
            pltpu.VMEM((n_ep * rows, model), bf16),
            pltpu.VMEM((n_ep // 2 * rows, model), bf16),
            pltpu.VMEM(((far - 1) * 2 * rows, model), bf16),
            pltpu.VMEM((rows, model), bf16),
            pltpu.VMEM((4 * rows, hidden_units), bf16),
            pltpu.VMEM((model, hidden_units), bf16),
            pltpu.VMEM((model, hidden_units), bf16),
            pltpu.VMEM((hidden_units, model), bf16),
            pltpu.SemaphoreType.DMA((n_copies,)),
            pltpu.SemaphoreType.DMA((n_copies,)),
            pltpu.SemaphoreType.DMA((3,)),
        ],
        compiler_params=pltpu.CompilerParams(
            collective_id=0, has_side_effects=True, vmem_limit_bytes=48 * 1024 * 1024
        ),
        cost_estimate=pl.CostEstimate(
            flops=6 * n_ep * rows * model * hidden_units,
            bytes_accessed=6 * model * hidden_units,
            transcendentals=0,
        ),
        name="expert_rings",
    )(block, hidden, w_gate, w_up, w_down)


def shards(
    hidden_in,
    queries,
    new_latents,
    cache,
    prefill_pool,
    requests,
    context_len,
    picks,
    w_uv,
    w_out,
    norm_gain,
    router,
    w_gate,
    w_up,
    w_down,
):
    n_ep = lax.axis_size("ep")
    steps, rows, share = hidden_in.shape
    heads, width = queries.shape[2], queries.shape[3]
    res, pool, top = cache.shape[0], prefill_pool.shape[0], picks.shape[2]
    experts, model = router.shape[1], router.shape[0]
    bf16 = jnp.bfloat16

    member = jnp.any(picks[..., None] == jnp.arange(experts), axis=2).astype(bf16)

    notes = 4 + experts
    extra = -(-(share + notes) // width)
    note = jnp.concatenate(
        [
            jnp.broadcast_to(
                jnp.stack(
                    [requests % pool + 1, context_len[res:] // 128, context_len[res:] % 128, jnp.arange(pool)],
                    axis=1,
                ).astype(bf16),
                (steps, pool, 4),
            ),
            member[:, res:],
            jnp.zeros((steps, pool, extra * width - share - notes), bf16),
        ],
        axis=2,
    )
    riders = jnp.concatenate([hidden_in[:, res:], note], axis=2).reshape(steps, pool, extra, width)
    packed = jnp.concatenate([queries[:, res:], new_latents[:, res:, None, :], riders], axis=2)
    to_owner = (jnp.arange(n_ep)[:, None] == (requests // pool)[None, :]).astype(bf16)
    outgoing = jnp.einsum("dk,tkhc->dthc", to_owner, packed, preferred_element_type=bf16)
    arrived = lax.all_to_all(outgoing, "ep", split_axis=0, concat_axis=0, tiled=True)
    slot_asked = arrived[:, 0, heads + 1 + share // width, share % width].astype(jnp.int32)
    from_asker = (slot_asked[None, :] == 1 + jnp.arange(pool)[:, None]).astype(bf16)
    taken = jnp.einsum("pe,ethc->tphc", from_asker, arrived, preferred_element_type=bf16)
    moved_queries = taken[:, :, :heads]
    moved_latents = taken[:, :, heads]
    riders = taken[:, :, heads + 1 :].reshape(steps, pool, extra * width)
    moved_hidden = riders[:, :, :share]
    ctx_parts = riders[0, :, share + 1 : share + 3].astype(jnp.int32)
    moved_ctx = ctx_parts[:, 0] * 128 + ctx_parts[:, 1]
    moved_member = riders[:, :, share + 4 : share + 4 + experts]
    asker_row = riders[:, :, share + 3] + (pool * jnp.arange(steps)[:, None]).astype(bf16)
    asker = jnp.broadcast_to(
        jnp.sum(from_asker * jnp.arange(n_ep).astype(bf16), axis=1), (steps, pool)
    )

    if lax.axis_size("tp") > 1:
        cache = lax.all_gather(cache, "tp", axis=1, tiled=True)
        prefill_pool = lax.all_gather(prefill_pool, "tp", axis=1, tiled=True)
    latent = jnp.concatenate(
        [
            attend_rows(queries[:, :res], new_latents[:, :res], cache, context_len[:res]),
            attend_rows(moved_queries, moved_latents, prefill_pool, moved_ctx),
        ],
        axis=1,
    )
    values = jnp.einsum("trhc,hcv->trhv", latent, w_uv, preferred_element_type=jnp.float32).astype(bf16)
    partial_value = jnp.einsum("trhv,hvd->trd", values, w_out, preferred_element_type=jnp.float32)
    hidden_rows = jnp.concatenate([hidden_in[:, :res], moved_hidden], axis=1).astype(jnp.float32)
    tp = lax.axis_index("tp")
    if lax.axis_size("tp") > 1:
        column = tp * share
        placed = lax.dynamic_update_slice_in_dim(jnp.zeros_like(partial_value), hidden_rows, column, 2)
        hidden = lax.psum(partial_value + placed, "tp")
        own_cols = lax.dynamic_slice_in_dim(hidden, column, share, 2)
    else:
        hidden = partial_value + hidden_rows
        own_cols = hidden
    scale = lax.rsqrt(jnp.mean(hidden * hidden, axis=-1, keepdims=True) + NORM_EPS)
    normed = (hidden * scale * norm_gain).astype(bf16)

    affinity = jax.nn.sigmoid(jnp.einsum("trd,de->tre", normed, router, preferred_element_type=jnp.float32))
    members = jnp.concatenate([member[:, :res], moved_member], axis=1)
    chosen = jnp.where(members > 0, affinity, 0.0)
    gates = chosen / jnp.sum(chosen, axis=-1, keepdims=True) * ROUTE_SCALE
    coarse = gates.astype(bf16)
    fine = (gates - coarse.astype(jnp.float32)).astype(bf16)
    address = jnp.stack([asker, asker_row], axis=-1)
    address = jnp.concatenate([jnp.zeros((steps, res, 2), bf16), address], axis=1)
    blank = jnp.zeros((steps, rows, 126 - 2 * experts), bf16)
    block = jnp.concatenate([normed, coarse, fine, address, blank], axis=2)
    wide = model + 128
    block = jnp.concatenate(
        [block[:, :res].reshape(steps * res, wide), block[:, res:].reshape(steps * pool, wide)], axis=0
    )
    moved_hidden = hidden[:, res:].reshape(steps * pool, model)
    if lax.axis_size("tp") > 1:
        moved_hidden = jnp.where(tp == 0, moved_hidden, 0.0)
    mixed = expert_rings(block, moved_hidden, w_gate, w_up, w_down, n_ep, lax.axis_size("tp") == 1)
    mixed = jnp.concatenate(
        [mixed[: steps * res].reshape(steps, res, model), mixed[steps * res :].reshape(steps, pool, model)], axis=1
    )
    if lax.axis_size("tp") > 1:
        mixed = lax.psum_scatter(mixed, "tp", scatter_dimension=2, tiled=True)
    resident = jnp.arange(rows)[None, :, None] < res
    return (jnp.where(resident, own_cols, 0.0) + mixed).astype(bf16)


def solution(mesh):
    in_specs = (
        P(None, ("group", "ep"), "tp"),
        P(None, ("group", "ep"), "tp", None),
        P(None, ("group", "ep"), None),
        P(("group", "ep"), "tp", None),
        P(("group", "ep"), "tp", None),
        P(("group", "ep")),
        P(("group", "ep")),
        P(None, ("group", "ep"), None),
        P("tp", None, None),
        P("tp", None, None),
        P(),
        P(),
        P("ep", None, "tp"),
        P("ep", None, "tp"),
        P("ep", "tp", None),
    )
    out_specs = P(None, ("group", "ep"), "tp")
    return jax.shard_map(shards, mesh=mesh, in_specs=in_specs, out_specs=out_specs, check_vma=False)
```
